128 devices in a mesh: work: 128 (over x, y, z, core).
Axes of the slice: x: 4, y: 4, z: 4, core: 2. Of those that a mesh axis runs over, the one named last changes fastest.
Arguments:
- embeddings: bfloat16 [65536, 1024], P('work'), may hold values from -6 to 6
- labels: int32 [65536, 1], P('work'), may hold values from 0 to 255; in each aligned block of 512 rows (0 to 511, 512 to 1023, ...) at most 4 rows name the same one
Outputs:
- nearest: float32 [65536], P('work')
The draws below stay inside these ranges and needn't reach their ends.
Inputs may be any that keep to these rules, and one draw needn't show every extreme that they name: `labels`: within the rows of one device no label occurs more than 4 times, and in every draw some label occurs exactly 4 times on some device; every label occurs somewhere.
All inputs are finite; a program needn't handle non-finite values.
Results may differ from the reference program's by a relative error of at most 0.0015.
Values may be sent and summed in bfloat16 or wider, within the bound.
No kernel may reach another device: no remote copies, remote signals or barrier semaphores. Data moves between devices by JAX's collectives and lax.ppermute only.
A program may use at most 64 MiB of HBM per device.

```python
import math
import jax
import jax.numpy as jnp
import numpy as np
from jax import lax

D = 1024
ROW_DEV = 512
ROWS = 65536
CLUSTERS = 256
MOST = 4
N_WORK = 128


def levels(key, shape, split, low, largest):
    gain = 1.0
    for position, blocks in split:
        heights = jax.random.uniform(jax.random.fold_in(jax.random.fold_in(key, 6), position), (blocks,), jnp.float32, low / len(split), largest / len(split))
        gain = gain * jnp.repeat(jnp.exp(heights), shape[position] // blocks).reshape((-1,) + (1,) * (len(shape) - 1 - position))
    return gain


def deal_out(stream_key, own, number, rows, amount, top, bound, skew):
    sequence = jax.random.permutation(stream_key, amount)
    crowded, ordinary = portions_of(amount, rows * top, bound, skew, True), portions_of(amount, rows * top, bound, skew, False)
    places = jnp.arange(amount)

    def named(tallies, turn):
        used = int((tallies > 0).sum())
        fixed = max(1, used // 4)
        moved = fixed + (places - fixed + turn * (used - fixed)) % max(1, amount - fixed)
        return jnp.zeros((amount,), jnp.int32).at[sequence[jnp.where(places < fixed, places, moved)]].set(jnp.asarray(tallies, jnp.int32))

    tallies = jnp.where(number % 4 == 0, named(crowded, number // 4), named(ordinary, number - number // 4 - 1))
    mixed = jax.random.permutation(jax.random.fold_in(own, 3), amount)
    giver, receiver = mixed[0:amount // 2 * 2:2], mixed[1:amount // 2 * 2:2]
    margin = jnp.minimum(tallies[giver] - 1, bound - tallies[receiver]) // 2
    margin = jnp.where((giver == sequence[0]) | (receiver == sequence[0]) | (tallies[receiver] == 0), 0, jnp.maximum(margin, 0))
    moved = jax.random.randint(jax.random.fold_in(own, 4), (amount // 2,), 0, 1 << 20) % (margin + 1)
    tallies = tallies.at[giver].add(-moved).at[receiver].add(moved)
    items = jnp.searchsorted(jnp.cumsum(tallies), jnp.arange(rows * top), side="right").astype(jnp.int32)
    listing = items.reshape(top, rows).T
    listing = listing[jax.random.permutation(jax.random.fold_in(own, 1), rows)]
    turn = jax.random.randint(jax.random.fold_in(own, 2), (rows, 1), 0, top)
    return jnp.take_along_axis(listing, (jnp.arange(top)[None, :] + turn) % top, axis=1)


def portions_of(amount, total, most, lean, full):
    loads = [(1 << 20) // math.isqrt(rank ** lean) + 1 for rank in range(1, amount + 1)]
    largest = most if full else min(most, max(-(-total // amount), total * loads[0] // sum(loads)))
    least = 1 if total - largest >= amount - 1 else 0
    given, spare = [largest] + [least] * (amount - 1), total - largest - least * (amount - 1)
    while spare > 0:
        candidates = [i for i in range(1, amount) if given[i] < largest] or [i for i in range(1, amount) if given[i] < most]
        mass, left = sum([loads[i] for i in candidates]), spare
        for i in candidates:
            more = min(most - given[i], max(1, left * loads[i] // mass), spare)
            given[i] = given[i] + more
            spare = spare - more
    return np.array(given)


def scatter_about(stream_key, extent, scale, most, shards=(), kind=jnp.bfloat16):
    array = jax.random.normal(stream_key, extent, jnp.float32) * scale
    if len(shards) > 0:
        array = levels(stream_key, extent, shards, -0.22, 0.18) * array
    return jnp.clip(array, min=-most, max=most).astype(kind)


def setup_inputs(seed: int = 0) -> dict:
    keys = jax.random.split(jax.random.key(seed), 3)
    embeddings = scatter_about(keys[0], (ROWS, D), 1.0, 6.0, ((0, 128),))
    labels_keys = jax.random.split(jax.random.fold_in(keys[1], 1), ROWS // ROW_DEV)
    labels_turns = jax.random.permutation(jax.random.fold_in(keys[1], 3), ROWS // ROW_DEV)
    labels = jax.vmap(lambda own, number: deal_out(jax.random.fold_in(keys[1], 2), own, number, ROW_DEV, CLUSTERS, 1, MOST, 2))(labels_keys, labels_turns).reshape((ROWS, 1))
    return dict(embeddings=embeddings, labels=labels)


def reference(embeddings, labels):
    label_row = labels[:, 0].astype(jnp.int32)
    values = embeddings.astype(jnp.float32)
    squares = lax.optimization_barrier(jnp.sum(values * values, axis=1, keepdims=True))
    unit = (values * lax.rsqrt(squares + 1e-06)).astype(jnp.bfloat16)
    order = jnp.argsort(label_row, stable=True).astype(jnp.int32)
    sorted_unit = unit[order].astype(jnp.float32)
    sorted_label = label_row[order]
    reach = N_WORK * MOST
    padded_unit = jnp.concatenate([sorted_unit, jnp.zeros((reach, D), jnp.float32)], axis=0)
    padded_label = jnp.concatenate([sorted_label, jnp.full((reach,), -1, jnp.int32)], axis=0)
    starts = jnp.searchsorted(sorted_label, jnp.arange(CLUSTERS, dtype=jnp.int32), side='left').astype(jnp.int32)
    local = jnp.arange(reach, dtype=jnp.int32)

    def one_cluster(index, found):
        start = starts[index].astype(jnp.int32)
        block = lax.dynamic_slice_in_dim(padded_unit, start, reach, 0)
        block_label = lax.dynamic_slice_in_dim(padded_label, start, reach, 0)
        live = block_label == index
        sim = jnp.dot(block, block.T, precision=lax.Precision.HIGHEST)
        usable = live[None, :] & (local[:, None] != local[None, :])
        best = lax.optimization_barrier(jnp.max(jnp.where(usable, sim, -1.0), axis=1))
        best = jnp.where(live, best, -2.0)
        return found.at[start + local].max(best)
    found = jnp.full((ROWS + reach,), -2.0, jnp.float32)
    found = lax.fori_loop(0, CLUSTERS, one_cluster, found)
    flat = found[:ROWS]
    return jnp.zeros((ROWS,), jnp.float32).at[order].set(flat)
```

```python
import jax
import jax.numpy as jnp
from jax import lax
from jax.experimental import pallas as pl
from jax.experimental.pallas import tpu as pltpu
from jax.sharding import PartitionSpec as P

CLUSTERS = 256
CL_DEV = 2
MOST = 4
PART = CL_DEV * MOST
DEAD = 4.0
LOW = -1e30


def iota(shape, dim):
    return lax.broadcasted_iota(jnp.int32, shape, dim)


def parts_of(values):
    out = []
    for _ in range(3):
        part = values.astype(jnp.bfloat16)
        out.append(part)
        values = values - part.astype(jnp.float32)
    return out


def dot(a, b, dims):
    return lax.dot_general(a, b, (dims, ((), ())), preferred_element_type=jnp.float32)


def place_kernel(label_ref, rows_ref, send_ref, slot_ref):
    rows, width = rows_ref.shape
    total = send_ref.shape[0]
    label = label_ref[...]
    member = iota((CLUSTERS, rows), 0) == label
    before = (iota((rows, rows), 0) < iota((rows, rows), 1)).astype(jnp.float32).astype(jnp.bfloat16)
    earlier = dot(member.astype(jnp.float32).astype(jnp.bfloat16), before, ((1,), (0,)))
    rank = jnp.sum(jnp.where(member, earlier, 0.0), axis=0, keepdims=True)
    slot = label * MOST + rank.astype(jnp.int32)
    slot_ref[...] = slot
    values = rows_ref[...].astype(jnp.float32)
    squares = jnp.sum(values * values, axis=1, keepdims=True)
    unit = (values * lax.rsqrt(squares + 1e-06)).astype(jnp.bfloat16)
    step = 256
    for first in range(0, total, step):
        chosen = (iota((step, rows), 0) + first == slot).astype(jnp.float32)
        empty = DEAD - DEAD * jnp.sum(chosen, axis=1, keepdims=True)
        placed = dot(chosen.astype(jnp.bfloat16), unit, ((1,), (0,)))
        send_ref[first : first + step, :128] = (placed[:, :128] + empty).astype(jnp.bfloat16)
        send_ref[first : first + step, 128:] = placed[:, 128:].astype(jnp.bfloat16)


def maxima_kernel(rows_ref, out_ref):
    total = rows_ref.shape[0]
    count = total // PART
    step = 256
    tile = 128
    same = (iota((step, tile), 0) & MOST) == (iota((step, tile), 1) & MOST)
    other = iota((tile, tile), 0) != iota((tile, tile), 1)
    best = jnp.full((8, total), -1.0, jnp.float32)
    for first in range(0, total, step):
        part = rows_ref[first : first + step, :]
        live = part[:, :1].astype(jnp.float32) < 0.5 * DEAD
        bias = jnp.where(same & live, 0.0, LOW)
        sim = dot(part, rows_ref[...], ((1,), (1,)))
        found = []
        for left in range(0, total, tile):
            block = sim[:, left : left + tile] + bias
            if first <= left < first + step:
                top = left - first
                pieces = [block[:top], jnp.where(other, block[top : top + tile], LOW), block[top + tile :]]
                block = jnp.concatenate([p for p in pieces if p.shape[0]], axis=0)
            found.append(jnp.max(block.reshape(step // 8, 8, tile), axis=0))
        best = jnp.maximum(best, jnp.concatenate(found, axis=1))
    best = jnp.max(best, axis=0, keepdims=True)
    mine = iota((count, total), 1) // PART == iota((count, total), 0)
    spread = (iota((total, 128), 0) % PART == iota((total, 128), 1) % PART).astype(jnp.float32).astype(jnp.bfloat16)
    out = jnp.zeros((count, 128), jnp.float32)
    for piece in parts_of(best):
        held = jnp.where(mine, piece.astype(jnp.float32), 0.0).astype(jnp.bfloat16)
        out = out + dot(held, spread, ((1,), (0,)))
    out_ref[...] = out


def lookup_kernel(slot_ref, found_ref, out_ref):
    rows = slot_ref.shape[1]
    count = found_ref.shape[0]
    slot = slot_ref[...]
    owner = (iota((count, rows), 0) == slot // PART).astype(jnp.float32).astype(jnp.bfloat16)
    picked = jnp.zeros((128, rows), jnp.float32)
    for piece in parts_of(found_ref[...]):
        picked = picked + dot(piece, owner, ((0,), (0,)))
    picked = picked[:PART]
    out_ref[...] = jnp.sum(jnp.where(iota((PART, rows), 0) == slot % PART, picked, 0.0), axis=0, keepdims=True)


def call(kernel, out_shape, name):
    return pl.pallas_call(
        kernel,
        out_shape=out_shape,
        compiler_params=pltpu.CompilerParams(vmem_limit_bytes=40 * 1024 * 1024),
        name=name,
    )


def exchange(array):
    return lax.all_to_all(array, "work", split_axis=0, concat_axis=0, tiled=True)


def local(embeddings, labels):
    count = lax.axis_size("work")
    rows, width = embeddings.shape
    total = count * PART
    send, slot = call(
        place_kernel,
        (jax.ShapeDtypeStruct((total, width), jnp.bfloat16), jax.ShapeDtypeStruct((1, rows), jnp.int32)),
        "place",
    )(labels.reshape(1, rows), embeddings)
    held = exchange(send.reshape(count, PART, width)).reshape(total, width)
    best = call(maxima_kernel, jax.ShapeDtypeStruct((count, 128), jnp.float32), "maxima")(held)
    found = exchange(best)
    nearest = call(lookup_kernel, jax.ShapeDtypeStruct((1, rows), jnp.float32), "lookup")(slot, found)
    return nearest.reshape(rows)


def solution(mesh):
    return jax.shard_map(
        local,
        mesh=mesh,
        in_specs=(P("work", None), P("work", None)),
        out_specs=P("work"),
        check_vma=False,
    )
```

```python
import jax
import jax.numpy as jnp
from jax import lax
from jax.experimental import pallas as pl
from jax.experimental.pallas import tpu as pltpu
from jax.sharding import PartitionSpec as P

CLUSTERS = 256
CL_DEV = 2
MOST = 4
PART = CL_DEV * MOST
DEAD = 4.0
LOW = -1e30
CHUNKS = 4
PARAMS = pltpu.CompilerParams(vmem_limit_bytes=40 * 1024 * 1024)


def iota(shape, dim):
    return lax.broadcasted_iota(jnp.int32, shape, dim)


def parts_of(values):
    out = []
    for _ in range(2):
        part = values.astype(jnp.bfloat16)
        out.append(part)
        values = values - part.astype(jnp.float32)
    return out


def bits(mask):
    return mask.astype(jnp.float32).astype(jnp.bfloat16)


def dot(a, b, dims):
    return lax.dot_general(a, b, (dims, ((), ())), preferred_element_type=jnp.float32)


def place_kernel(label_hbm, rows_hbm, send_ref, slot_ref, label_ref, rows_ref, unit_ref, chosen_ref, label_sem, rows_sem):
    rows = rows_ref.shape[0]
    total = send_ref.shape[0]
    chunk = rows // CHUNKS
    label_copy = pltpu.make_async_copy(label_hbm, label_ref, label_sem)
    label_copy.start()
    copies = []
    for index in range(CHUNKS):
        part = pl.ds(index * chunk, chunk)
        copies.append(pltpu.make_async_copy(rows_hbm.at[part], rows_ref.at[part], rows_sem.at[index]))
        copies[-1].start()
    before = bits(iota((rows, rows), 0) < iota((rows, rows), 1))
    label_copy.wait()
    label = label_ref[...]
    member = iota((CLUSTERS, rows), 0) == label
    earlier = dot(bits(member), before, ((1,), (0,)))
    rank = jnp.sum(jnp.where(member, earlier, 0.0), axis=0, keepdims=True)
    slot = label * MOST + rank.astype(jnp.int32)
    slot_ref[...] = slot
    step = 256
    empty = []
    for first in range(0, total, step):
        chosen = (iota((step, rows), 0) + first == slot).astype(jnp.float32)
        empty.append(DEAD - DEAD * jnp.sum(chosen, axis=1, keepdims=True))
        chosen_ref[first : first + step, :] = chosen.astype(jnp.bfloat16)
    for index in range(CHUNKS):
        part = pl.ds(index * chunk, chunk)
        copies[index].wait()
        values = rows_ref[part, :].astype(jnp.float32)
        squares = jnp.sum(values * values, axis=1, keepdims=True)
        unit_ref[part, :] = (values * lax.rsqrt(squares + 1e-06)).astype(jnp.bfloat16)
    for first in range(0, total, step):
        placed = dot(chosen_ref[first : first + step, :], unit_ref[...], ((1,), (0,)))
        send_ref[first : first + step, :128] = (placed[:, :128] + empty[first // step]).astype(jnp.bfloat16)
        send_ref[first : first + step, 128:] = placed[:, 128:].astype(jnp.bfloat16)


def maxima_kernel(rows_ref, out_ref):
    total = rows_ref.shape[0]
    count = total // PART
    step = 256
    blocks = total // step
    tile = 128
    same = (iota((step, tile), 0) & MOST) == (iota((step, tile), 1) & MOST)
    other = iota((step, step), 0) != iota((step, step), 1)
    empty = [rows_ref[b * step : (b + 1) * step, :tile].astype(jnp.float32) for b in range(blocks)]
    down = [jnp.where(same & (e[:, :1] < 0.5 * DEAD), 0.0, LOW) for e in empty]
    across = [jnp.where(jnp.transpose(e)[:1] < 0.5 * DEAD, 0.0, LOW) for e in empty]
    over_rows = [jnp.full((8, step), -1.0, jnp.float32) for _ in range(blocks)]
    over_columns = [jnp.full((step, tile), -1.0, jnp.float32) for _ in range(blocks)]
    for i in range(blocks):
        for j in range(i, blocks):
            sim = dot(rows_ref[i * step : (i + 1) * step, :], rows_ref[j * step : (j + 1) * step, :], ((1,), (1,)))
            sim = sim + jnp.concatenate([down[i]] * (step // tile), axis=1)
            if i == j:
                sim = jnp.where(other, sim, LOW)
            else:
                sim = sim + across[j]
                for left in range(0, step, tile):
                    over_columns[i] = jnp.maximum(over_columns[i], sim[:, left : left + tile])
            over_rows[j] = jnp.maximum(over_rows[j], jnp.max(sim.reshape(step // 8, 8, step), axis=0))
    best = jnp.max(jnp.concatenate(over_rows, axis=1), axis=0, keepdims=True)
    rest = jnp.max(jnp.concatenate(over_columns, axis=0), axis=1, keepdims=True)
    mine = iota((count, total), 1) // PART == iota((count, total), 0)
    spread = iota((total, tile), 0) % PART == iota((total, tile), 1) % PART
    mine_one, spread_one = bits(mine), bits(spread)
    one = jnp.zeros((count, tile), jnp.float32)
    for piece in parts_of(best):
        one = one + dot(jnp.where(mine, piece.astype(jnp.float32), 0.0).astype(jnp.bfloat16), spread_one, ((1,), (0,)))
    two = jnp.zeros((count, tile), jnp.float32)
    for piece in parts_of(rest):
        two = two + dot(mine_one, jnp.where(spread, piece.astype(jnp.float32), 0.0).astype(jnp.bfloat16), ((1,), (0,)))
    out_ref[...] = jnp.maximum(one, two)


def lookup_kernel(slot_ref, found_ref, out_ref):
    rows = slot_ref.shape[1]
    count = found_ref.shape[0]
    slot = slot_ref[...]
    owner = bits(iota((count, rows), 0) == slot // PART)
    picked = jnp.zeros((128, rows), jnp.float32)
    for piece in parts_of(found_ref[...]):
        picked = picked + dot(piece, owner, ((0,), (0,)))
    picked = picked[:PART]
    out_ref[...] = jnp.sum(jnp.where(iota((PART, rows), 0) == slot % PART, picked, 0.0), axis=0, keepdims=True)


def call(kernel, out_shape, name):
    return pl.pallas_call(
        kernel,
        out_shape=out_shape,
        compiler_params=PARAMS,
        name=name,
    )


def exchange(array):
    return lax.all_to_all(array, "work", split_axis=0, concat_axis=0, tiled=True)


def local(embeddings, labels):
    count = lax.axis_size("work")
    rows, width = embeddings.shape
    total = count * PART
    send, slot = pl.pallas_call(
        place_kernel,
        out_shape=(jax.ShapeDtypeStruct((total, width), jnp.bfloat16), jax.ShapeDtypeStruct((1, rows), jnp.int32)),
        in_specs=[pl.BlockSpec(memory_space=pltpu.HBM)] * 2,
        scratch_shapes=[
            pltpu.VMEM((1, rows), jnp.int32),
            pltpu.VMEM((rows, width), jnp.bfloat16),
            pltpu.VMEM((rows, width), jnp.bfloat16),
            pltpu.VMEM((total, rows), jnp.bfloat16),
            pltpu.SemaphoreType.DMA,
            pltpu.SemaphoreType.DMA((CHUNKS,)),
        ],
        compiler_params=pltpu.CompilerParams(vmem_limit_bytes=40 * 1024 * 1024),
        name="place",
    )(
        pltpu.with_memory_space_constraint(labels.reshape(1, rows), pltpu.HBM),
        pltpu.with_memory_space_constraint(embeddings, pltpu.HBM),
    )
    held = exchange(send.reshape(count, PART, width)).reshape(total, width)
    best = call(maxima_kernel, jax.ShapeDtypeStruct((count, 128), jnp.float32), "maxima")(held)
    found = exchange(best)
    nearest = call(lookup_kernel, jax.ShapeDtypeStruct((1, rows), jnp.float32), "lookup")(slot, found)
    return nearest.reshape(rows)


def solution(mesh):
    return jax.shard_map(
        local,
        mesh=mesh,
        in_specs=(P("work", None), P("work", None)),
        out_specs=P("work"),
        check_vma=False,
    )
```

```python
import jax
import jax.numpy as jnp
from jax import lax
from jax.experimental import pallas as pl
from jax.experimental.pallas import tpu as pltpu
from jax.sharding import PartitionSpec as P

CLUSTERS = 256
CL_DEV = 2
MOST = 4
PART = CL_DEV * MOST
MARK = 2.0**-126
LOW = -1e30
CHUNKS = 1
PARAMS = pltpu.CompilerParams(vmem_limit_bytes=40 * 1024 * 1024)


def iota(shape, dim):
    return lax.broadcasted_iota(jnp.int32, shape, dim)


def parts_of(values):
    out = []
    for _ in range(2):
        part = values.astype(jnp.bfloat16)
        out.append(part)
        values = values - part.astype(jnp.float32)
    return out


def bits(mask):
    return mask.astype(jnp.float32).astype(jnp.bfloat16)


def dot(a, b, dims):
    return lax.dot_general(a, b, (dims, ((), ())), preferred_element_type=jnp.float32)


def place_kernel(label_hbm, rows_hbm, send_ref, slot_ref, label_ref, rows_ref, unit_ref, chosen_ref, label_sem, rows_sem):
    rows = rows_ref.shape[0]
    total = send_ref.shape[0]
    chunk = rows // CHUNKS
    label_copy = pltpu.make_async_copy(label_hbm, label_ref, label_sem)
    label_copy.start()
    copies = []
    for index in range(CHUNKS):
        part = pl.ds(index * chunk, chunk)
        copies.append(pltpu.make_async_copy(rows_hbm.at[part], rows_ref.at[part], rows_sem.at[index]))
        copies[-1].start()
    before = bits(iota((rows, rows), 0) < iota((rows, rows), 1))
    label_copy.wait()
    label = label_ref[...]
    member = iota((CLUSTERS, rows), 0) == label
    earlier = dot(bits(member), before, ((1,), (0,)))
    rank = jnp.sum(jnp.where(member, earlier, 0.0), axis=0, keepdims=True)
    slot = label * MOST + rank.astype(jnp.int32)
    slot_ref[...] = slot
    step = 256
    for first in range(0, total, step):
        chosen_ref[first : first + step, :] = bits(iota((step, rows), 0) + first == slot)
    first_lane = iota((chunk, 128), 1) == 0
    for index in range(CHUNKS):
        part = pl.ds(index * chunk, chunk)
        copies[index].wait()
        values = rows_ref[part, :].astype(jnp.float32)
        squares = values * values
        folded = squares[:, :128]
        for left in range(128, rows_ref.shape[1], 128):
            folded = folded + squares[:, left : left + 128]
        squares = jnp.sum(folded, axis=1, keepdims=True)
        unit = values * lax.rsqrt(squares + 1e-06)
        head = unit[:, :128]
        unit_ref[part, :128] = jnp.where((jnp.abs(head) < MARK) & first_lane, MARK, head).astype(jnp.bfloat16)
        unit_ref[part, 128:] = unit[:, 128:].astype(jnp.bfloat16)
    for left in range(0, rows_ref.shape[1], step):
        placed = dot(chosen_ref[...], unit_ref[:, left : left + step], ((1,), (0,)))
        send_ref[:, left : left + step] = placed.astype(jnp.bfloat16)


def maxima_kernel(rows_ref, out_ref):
    total = rows_ref.shape[0]
    count = total // PART
    step = 256
    blocks = total // step
    tile = 128
    same = (iota((step, tile), 0) & MOST) == (iota((step, tile), 1) & MOST)
    other = iota((step, step), 0) != iota((step, step), 1)
    empty = [rows_ref[b * step : (b + 1) * step, :tile].astype(jnp.float32) for b in range(blocks)]
    down = [jnp.where(same & (e[:, :1] != 0.0), 0.0, LOW) for e in empty]
    across = [jnp.where(jnp.transpose(e)[:1] != 0.0, 0.0, LOW) for e in empty]
    over_rows = [jnp.full((8, step), -1.0, jnp.float32) for _ in range(blocks)]
    over_columns = [jnp.full((step, tile), -1.0, jnp.float32) for _ in range(blocks)]
    for i in range(blocks):
        for j in range(i, blocks):
            sim = dot(rows_ref[i * step : (i + 1) * step, :], rows_ref[j * step : (j + 1) * step, :], ((1,), (1,)))
            sim = sim + jnp.concatenate([down[i]] * (step // tile), axis=1)
            if i == j:
                sim = jnp.where(other, sim, LOW)
            else:
                sim = sim + across[j]
                for left in range(0, step, tile):
                    over_columns[i] = jnp.maximum(over_columns[i], sim[:, left : left + tile])
            over_rows[j] = jnp.maximum(over_rows[j], jnp.max(sim.reshape(step // 8, 8, step), axis=0))
    best = []
    for over_row, over_column in zip(over_rows, over_columns):
        column = jnp.max(jnp.transpose(over_column), axis=0, keepdims=True)
        best.append(jnp.maximum(jnp.max(over_row, axis=0, keepdims=True), column))
    best = jnp.concatenate(best, axis=1)
    best = jnp.concatenate([best[:, left : left + tile] for left in range(0, total, tile)], axis=0)
    for place in range(tile // PART):
        out_ref[pl.ds(place, total // tile, stride=tile // PART), :] = pltpu.roll(best, -place * PART % tile, axis=1)


def lookup_kernel(slot_ref, found_ref, out_ref):
    rows = slot_ref.shape[1]
    count = found_ref.shape[0]
    slot = slot_ref[...]
    owner = bits(iota((count, rows), 0) == slot // PART)
    picked = jnp.zeros((128, rows), jnp.float32)
    for piece in parts_of(found_ref[...]):
        picked = picked + dot(piece, owner, ((0,), (0,)))
    picked = picked[:PART]
    out_ref[...] = jnp.sum(jnp.where(iota((PART, rows), 0) == slot % PART, picked, 0.0), axis=0, keepdims=True)


def call(kernel, out_shape, name):
    return pl.pallas_call(
        kernel,
        out_shape=out_shape,
        compiler_params=PARAMS,
        name=name,
    )


def exchange(array):
    return lax.all_to_all(array, "work", split_axis=0, concat_axis=0, tiled=True)


def local(embeddings, labels):
    count = lax.axis_size("work")
    rows, width = embeddings.shape
    total = count * PART
    send, slot = pl.pallas_call(
        place_kernel,
        out_shape=(jax.ShapeDtypeStruct((total, width), jnp.bfloat16), jax.ShapeDtypeStruct((1, rows), jnp.int32)),
        in_specs=[pl.BlockSpec(memory_space=pltpu.HBM)] * 2,
        scratch_shapes=[
            pltpu.VMEM((1, rows), jnp.int32),
            pltpu.VMEM((rows, width), jnp.bfloat16),
            pltpu.VMEM((rows, width), jnp.bfloat16),
            pltpu.VMEM((total, rows), jnp.bfloat16),
            pltpu.SemaphoreType.DMA,
            pltpu.SemaphoreType.DMA((CHUNKS,)),
        ],
        compiler_params=pltpu.CompilerParams(vmem_limit_bytes=40 * 1024 * 1024),
        name="place",
    )(
        pltpu.with_memory_space_constraint(labels.reshape(1, rows), pltpu.HBM),
        pltpu.with_memory_space_constraint(embeddings, pltpu.HBM),
    )
    held = exchange(send.reshape(count, PART, width)).reshape(total, width)
    best = call(maxima_kernel, jax.ShapeDtypeStruct((count, 128), jnp.float32), "maxima")(held)
    found = exchange(best)
    nearest = call(lookup_kernel, jax.ShapeDtypeStruct((1, rows), jnp.float32), "lookup")(slot, found)
    return nearest.reshape(rows)


def solution(mesh):
    return jax.shard_map(
        local,
        mesh=mesh,
        in_specs=(P("work", None), P("work", None)),
        out_specs=P("work"),
        check_vma=False,
    )
```

```python
import jax
import jax.numpy as jnp
from jax import lax
from jax.experimental import pallas as pl
from jax.experimental.pallas import tpu as pltpu
from jax.sharding import PartitionSpec as P

CLUSTERS = 256
CL_DEV = 2
MOST = 4
PART = CL_DEV * MOST
MARK = 2.0**-126
LOW = -1e30
CHUNKS = 1
PARAMS = pltpu.CompilerParams(vmem_limit_bytes=40 * 1024 * 1024)


def iota(shape, dim):
    return lax.broadcasted_iota(jnp.int32, shape, dim)


def parts_of(values):
    out = []
    for _ in range(2):
        part = values.astype(jnp.bfloat16)
        out.append(part)
        values = values - part.astype(jnp.float32)
    return out


def bits(mask):
    return mask.astype(jnp.float32).astype(jnp.bfloat16)


def dot(a, b, dims):
    return lax.dot_general(a, b, (dims, ((), ())), preferred_element_type=jnp.float32)


def place_kernel(label_hbm, rows_hbm, send_ref, slot_ref, label_ref, rows_ref, unit_ref, chosen_ref, label_sem, rows_sem):
    rows = rows_ref.shape[0]
    total = send_ref.shape[0]
    chunk = rows // CHUNKS
    label_copy = pltpu.make_async_copy(label_hbm, label_ref, label_sem)
    label_copy.start()
    copies = []
    for index in range(CHUNKS):
        part = pl.ds(index * chunk, chunk)
        copies.append(pltpu.make_async_copy(rows_hbm.at[part], rows_ref.at[part], rows_sem.at[index]))
        copies[-1].start()
    before = bits(iota((rows, rows), 0) < iota((rows, rows), 1))
    label_copy.wait()
    label = label_ref[...]
    member = iota((CLUSTERS, rows), 0) == label
    earlier = dot(bits(member), before, ((1,), (0,)))
    rank = jnp.sum(jnp.where(member, earlier, 0.0), axis=0, keepdims=True)
    slot = (label * MOST + rank.astype(jnp.int32)) ^ ((lax.axis_index("work") & 2) * (MOST // 2))
    slot_ref[...] = slot
    step = 256
    for first in range(0, total, step):
        chosen_ref[first : first + step, :] = bits(iota((step, rows), 0) + first == slot)
    first_lane = iota((chunk, 128), 1) == 0
    for index in range(CHUNKS):
        part = pl.ds(index * chunk, chunk)
        copies[index].wait()
        values = rows_ref[part, :].astype(jnp.float32)
        squares = values * values
        folded = squares[:, :128]
        for left in range(128, rows_ref.shape[1], 128):
            folded = folded + squares[:, left : left + 128]
        squares = jnp.sum(folded, axis=1, keepdims=True)
        unit = values * lax.rsqrt(squares + 1e-06)
        head = unit[:, :128]
        unit_ref[part, :128] = jnp.where((jnp.abs(head) < MARK) & first_lane, MARK, head).astype(jnp.bfloat16)
        unit_ref[part, 128:] = unit[:, 128:].astype(jnp.bfloat16)
    for left in range(0, rows_ref.shape[1], step):
        placed = dot(chosen_ref[...], unit_ref[:, left : left + step], ((1,), (0,)))
        send_ref[:, left : left + step] = placed.astype(jnp.bfloat16)


def maxima_kernel(rows_ref, out_ref, left_ref, right_ref):
    total, width = rows_ref.shape
    half = total // CL_DEV
    step = 256
    blocks = half // step
    tile = 128
    upper = iota((16, width), 0) & MOST == 0
    for group in range(total // 32):
        one = rows_ref[group * 32 : group * 32 + 16, :]
        two = rows_ref[group * 32 + 16 : group * 32 + 32, :]
        left_ref[group * 16 : group * 16 + 16, :] = jnp.where(upper, one, two)
        right_ref[group * 16 : group * 16 + 16, :] = jnp.where(upper, two, one)
    other = iota((step, step), 0) != iota((step, step), 1)
    found = []
    for held in (left_ref, right_ref):
        mark = [held[b * step : (b + 1) * step, :tile].astype(jnp.float32) for b in range(blocks)]
        down = [jnp.where(m[:, :1] != 0.0, 0.0, LOW) for m in mark]
        across = [jnp.where(jnp.transpose(m)[:1] != 0.0, 0.0, LOW) for m in mark]
        over_rows = [jnp.full((8, step), -1.0, jnp.float32) for _ in range(blocks)]
        over_columns = [jnp.full((step, tile), -1.0, jnp.float32) for _ in range(blocks)]
        for i in range(blocks):
            for j in range(i, blocks):
                sim = dot(held[i * step : (i + 1) * step, :], held[j * step : (j + 1) * step, :], ((1,), (1,)))
                sim = sim + down[i]
                if i == j:
                    sim = jnp.where(other, sim, LOW)
                else:
                    sim = sim + across[j]
                    for first in range(0, step, tile):
                        over_columns[i] = jnp.maximum(over_columns[i], sim[:, first : first + tile])
                over_rows[j] = jnp.maximum(over_rows[j], jnp.max(sim.reshape(step // 8, 8, step), axis=0))
        best = []
        for over_row, over_column in zip(over_rows, over_columns):
            column = jnp.max(jnp.transpose(over_column), axis=0, keepdims=True)
            best.append(jnp.maximum(jnp.max(over_row, axis=0, keepdims=True), column))
        best = jnp.concatenate(best, axis=1)
        found.append(jnp.concatenate([best[:, first : first + tile] for first in range(0, half, tile)], axis=0))
    first_half = iota(found[0].shape, 1) & MOST == 0
    best = jnp.concatenate([jnp.where(first_half, found[0], found[1]), jnp.where(first_half, found[1], found[0])], axis=0)
    lines = half // tile
    for place in range(tile // PART):
        turned = pltpu.roll(best, -place * PART % tile, axis=1)
        row = place // 2 * 4 + place % 2
        out_ref[pl.ds(row, lines, stride=32), :] = turned[:lines]
        out_ref[pl.ds(row + 2, lines, stride=32), :] = turned[lines:]


def lookup_kernel(slot_ref, found_ref, out_ref):
    rows = slot_ref.shape[1]
    count = found_ref.shape[0]
    slot = slot_ref[...]
    owner = bits(iota((count, rows), 0) == slot // PART)
    picked = jnp.zeros((128, rows), jnp.float32)
    for piece in parts_of(found_ref[...]):
        picked = picked + dot(piece, owner, ((0,), (0,)))
    picked = picked[:PART]
    out_ref[...] = jnp.sum(jnp.where(iota((PART, rows), 0) == slot % PART, picked, 0.0), axis=0, keepdims=True)


def call(kernel, out_shape, name):
    return pl.pallas_call(
        kernel,
        out_shape=out_shape,
        compiler_params=PARAMS,
        name=name,
    )


def exchange(array):
    return lax.all_to_all(array, "work", split_axis=0, concat_axis=0, tiled=True)


def local(embeddings, labels):
    count = lax.axis_size("work")
    rows, width = embeddings.shape
    total = count * PART
    send, slot = pl.pallas_call(
        place_kernel,
        out_shape=(jax.ShapeDtypeStruct((total, width), jnp.bfloat16), jax.ShapeDtypeStruct((1, rows), jnp.int32)),
        in_specs=[pl.BlockSpec(memory_space=pltpu.HBM)] * 2,
        scratch_shapes=[
            pltpu.VMEM((1, rows), jnp.int32),
            pltpu.VMEM((rows, width), jnp.bfloat16),
            pltpu.VMEM((rows, width), jnp.bfloat16),
            pltpu.VMEM((total, rows), jnp.bfloat16),
            pltpu.SemaphoreType.DMA,
            pltpu.SemaphoreType.DMA((CHUNKS,)),
        ],
        compiler_params=pltpu.CompilerParams(vmem_limit_bytes=40 * 1024 * 1024),
        name="place",
    )(
        pltpu.with_memory_space_constraint(labels.reshape(1, rows), pltpu.HBM),
        pltpu.with_memory_space_constraint(embeddings, pltpu.HBM),
    )
    held = exchange(send.reshape(count, PART, width)).reshape(total, width)
    best = pl.pallas_call(
        maxima_kernel,
        out_shape=jax.ShapeDtypeStruct((count, 128), jnp.float32),
        scratch_shapes=[pltpu.VMEM((total // CL_DEV, width), jnp.bfloat16)] * CL_DEV,
        compiler_params=PARAMS,
        name="maxima",
    )(held)
    found = exchange(best)
    nearest = call(lookup_kernel, jax.ShapeDtypeStruct((1, rows), jnp.float32), "lookup")(slot, found)
    return nearest.reshape(rows)


def solution(mesh):
    return jax.shard_map(
        local,
        mesh=mesh,
        in_specs=(P("work", None), P("work", None)),
        out_specs=P("work"),
        check_vma=False,
    )
```

```python
import jax
import jax.numpy as jnp
from jax import lax
from jax.experimental import pallas as pl
from jax.experimental.pallas import tpu as pltpu
from jax.sharding import PartitionSpec as P

CLUSTERS = 256
CL_DEV = 2
MOST = 4
PART = CL_DEV * MOST
MARK = 2.0**-126
LOW = -1e30
CHUNKS = 1
PARAMS = pltpu.CompilerParams(vmem_limit_bytes=40 * 1024 * 1024)


def iota(shape, dim):
    return lax.broadcasted_iota(jnp.int32, shape, dim)


def parts_of(values):
    out = []
    for _ in range(2):
        part = values.astype(jnp.bfloat16)
        out.append(part)
        values = values - part.astype(jnp.float32)
    return out


def bits(mask):
    return mask.astype(jnp.float32).astype(jnp.bfloat16)


def dot(a, b, dims):
    return lax.dot_general(a, b, (dims, ((), ())), preferred_element_type=jnp.float32)


def place_kernel(label_hbm, rows_hbm, send_ref, slot_ref, label_ref, rows_ref, unit_ref, chosen_ref, label_sem, rows_sem):
    rows = rows_ref.shape[0]
    total = send_ref.shape[0]
    chunk = rows // CHUNKS
    label_copy = pltpu.make_async_copy(label_hbm, label_ref, label_sem)
    label_copy.start()
    copies = []
    for index in range(CHUNKS):
        part = pl.ds(index * chunk, chunk)
        copies.append(pltpu.make_async_copy(rows_hbm.at[part], rows_ref.at[part], rows_sem.at[index]))
        copies[-1].start()
    before = bits(iota((rows, rows), 0) < iota((rows, rows), 1))
    label_copy.wait()
    label = label_ref[...]
    member = iota((CLUSTERS, rows), 0) == label
    earlier = dot(bits(member), before, ((1,), (0,)))
    rank = jnp.sum(jnp.where(member, earlier, 0.0), axis=0, keepdims=True)
    slot = (label * MOST + rank.astype(jnp.int32)) ^ ((lax.axis_index("work") & 2) * (MOST // 2))
    slot_ref[...] = slot
    step = 256
    for first in range(0, total, step):
        chosen_ref[first : first + step, :] = bits(iota((step, rows), 0) + first == slot)
    first_lane = iota((chunk, 128), 1) == 0
    for index in range(CHUNKS):
        part = pl.ds(index * chunk, chunk)
        copies[index].wait()
        values = rows_ref[part, :].astype(jnp.float32)
        squares = values * values
        folded = squares[:, :128]
        for left in range(128, rows_ref.shape[1], 128):
            folded = folded + squares[:, left : left + 128]
        squares = jnp.sum(folded, axis=1, keepdims=True)
        unit = values * lax.rsqrt(squares + 1e-06)
        head = unit[:, :128]
        unit_ref[part, :128] = jnp.where((jnp.abs(head) < MARK) & first_lane, MARK, head).astype(jnp.bfloat16)
        unit_ref[part, 128:] = unit[:, 128:].astype(jnp.bfloat16)
    for left in range(0, rows_ref.shape[1], step):
        placed = dot(chosen_ref[...], unit_ref[:, left : left + step], ((1,), (0,)))
        send_ref[:, left : left + step] = placed.astype(jnp.bfloat16)


def maxima_kernel(rows_ref, out_ref, left_ref, right_ref):
    total, width = rows_ref.shape
    count = out_ref.shape[0]
    half = total // CL_DEV
    step = 256
    blocks = half // step
    tile = 128
    upper = iota((16, width), 0) & MOST == 0
    for group in range(total // 32):
        one = rows_ref[group * 32 : group * 32 + 16, :]
        two = rows_ref[group * 32 + 16 : group * 32 + 32, :]
        left_ref[group * 16 : group * 16 + 16, :] = jnp.where(upper, one, two)
        right_ref[group * 16 : group * 16 + 16, :] = jnp.where(upper, two, one)
    other = iota((step, step), 0) != iota((step, step), 1)
    found = []
    for held in (left_ref, right_ref):
        mark = [held[b * step : (b + 1) * step, :tile].astype(jnp.float32) for b in range(blocks)]
        down = [jnp.where(m[:, :1] != 0.0, 0.0, LOW) for m in mark]
        across = [jnp.where(jnp.transpose(m)[:1] != 0.0, 0.0, LOW) for m in mark]
        over_rows = [jnp.full((8, step), -1.0, jnp.float32) for _ in range(blocks)]
        over_columns = [jnp.full((step, tile), -1.0, jnp.float32) for _ in range(blocks)]
        for i in range(blocks):
            for j in range(i, blocks):
                sim = dot(held[i * step : (i + 1) * step, :], held[j * step : (j + 1) * step, :], ((1,), (1,)))
                sim = sim + down[i]
                if i == j:
                    sim = jnp.where(other, sim, LOW)
                else:
                    sim = sim + across[j]
                    for first in range(0, step, tile):
                        over_columns[i] = jnp.maximum(over_columns[i], sim[:, first : first + tile])
                over_rows[j] = jnp.maximum(over_rows[j], jnp.max(sim.reshape(step // 8, 8, step), axis=0))
        best = []
        for over_row, over_column in zip(over_rows, over_columns):
            column = jnp.max(jnp.transpose(over_column), axis=0, keepdims=True)
            best.append(jnp.maximum(jnp.max(over_row, axis=0, keepdims=True), column))
        tiles = [row[:, first : first + tile] for row in best for first in range(0, step, tile)]
        found.append(jnp.concatenate([t for row in tiles for t in (row, pltpu.roll(row, tile // 2, axis=1))], axis=0))
    first_half = iota(found[0].shape, 1) & MOST == 0
    lines = found[0].shape[0]
    apart = count // lines
    for swap in range(CL_DEV):
        best = jnp.where(first_half, found[swap], found[1 - swap])
        for place in range(tile // 2 // PART):
            row = place // 2 * 4 + swap * 2 + place % 2
            out_ref[pl.ds(row, lines, stride=apart), :] = pltpu.roll(best, -place * PART % tile, axis=1)


def lookup_kernel(slot_ref, found_ref, out_ref):
    rows = slot_ref.shape[1]
    count = found_ref.shape[0]
    slot = slot_ref[...]
    owner = bits(iota((count, rows), 0) == slot // PART)
    picked = jnp.zeros((128, rows), jnp.float32)
    for piece in parts_of(found_ref[...]):
        picked = picked + dot(piece, owner, ((0,), (0,)))
    picked = picked[:PART]
    out_ref[...] = jnp.sum(jnp.where(iota((PART, rows), 0) == slot % PART, picked, 0.0), axis=0, keepdims=True)


def call(kernel, out_shape, name):
    return pl.pallas_call(
        kernel,
        out_shape=out_shape,
        compiler_params=PARAMS,
        name=name,
    )


def exchange(array):
    return lax.all_to_all(array, "work", split_axis=0, concat_axis=0, tiled=True)


def local(embeddings, labels):
    count = lax.axis_size("work")
    rows, width = embeddings.shape
    total = count * PART
    send, slot = pl.pallas_call(
        place_kernel,
        out_shape=(jax.ShapeDtypeStruct((total, width), jnp.bfloat16), jax.ShapeDtypeStruct((1, rows), jnp.int32)),
        in_specs=[pl.BlockSpec(memory_space=pltpu.HBM)] * 2,
        scratch_shapes=[
            pltpu.VMEM((1, rows), jnp.int32),
            pltpu.VMEM((rows, width), jnp.bfloat16),
            pltpu.VMEM((rows, width), jnp.bfloat16),
            pltpu.VMEM((total, rows), jnp.bfloat16),
            pltpu.SemaphoreType.DMA,
            pltpu.SemaphoreType.DMA((CHUNKS,)),
        ],
        compiler_params=pltpu.CompilerParams(vmem_limit_bytes=40 * 1024 * 1024),
        name="place",
    )(
        pltpu.with_memory_space_constraint(labels.reshape(1, rows), pltpu.HBM),
        pltpu.with_memory_space_constraint(embeddings, pltpu.HBM),
    )
    held = exchange(send.reshape(count, PART, width)).reshape(total, width)
    best = pl.pallas_call(
        maxima_kernel,
        out_shape=jax.ShapeDtypeStruct((count, 128), jnp.float32),
        scratch_shapes=[pltpu.VMEM((total // CL_DEV, width), jnp.bfloat16)] * CL_DEV,
        compiler_params=PARAMS,
        name="maxima",
    )(held)
    found = exchange(best)
    nearest = call(lookup_kernel, jax.ShapeDtypeStruct((1, rows), jnp.float32), "lookup")(slot, found)
    return nearest.reshape(rows)


def solution(mesh):
    return jax.shard_map(
        local,
        mesh=mesh,
        in_specs=(P("work", None), P("work", None)),
        out_specs=P("work"),
        check_vma=False,
    )
```

```python
import jax
import jax.numpy as jnp
from jax import lax
from jax.experimental import pallas as pl
from jax.experimental.pallas import tpu as pltpu
from jax.sharding import PartitionSpec as P

CLUSTERS = 256
CL_DEV = 2
MOST = 4
PART = CL_DEV * MOST
MARK = 2.0**-126
LOW = -1e30
PARAMS = pltpu.CompilerParams(vmem_limit_bytes=40 * 1024 * 1024)


def iota(shape, dim):
    return lax.broadcasted_iota(jnp.int32, shape, dim)


def parts_of(values):
    out = []
    for _ in range(2):
        part = values.astype(jnp.bfloat16)
        out.append(part)
        values = values - part.astype(jnp.float32)
    return out


def bits(mask):
    return mask.astype(jnp.float32).astype(jnp.bfloat16)


def dot(a, b, dims):
    return lax.dot_general(a, b, (dims, ((), ())), preferred_element_type=jnp.float32)


def place_kernel(label_hbm, rows_hbm, send_ref, slot_ref, label_ref, rows_ref, unit_ref, chosen_ref, label_sem, rows_sem):
    rows = rows_ref.shape[0]
    total = send_ref.shape[0]
    label_copy = pltpu.make_async_copy(label_hbm, label_ref, label_sem)
    label_copy.start()
    rows_copy = pltpu.make_async_copy(rows_hbm, rows_ref, rows_sem)
    rows_copy.start()
    before = bits(iota((rows, rows), 0) < iota((rows, rows), 1))
    label_copy.wait()
    label = label_ref[...]
    member = iota((CLUSTERS, rows), 0) == label
    earlier = dot(bits(member), before, ((1,), (0,)))
    rank = jnp.sum(jnp.where(member, earlier, 0.0), axis=0, keepdims=True)
    slot = (label * MOST + rank.astype(jnp.int32)) ^ ((lax.axis_index("work") & 2) * (MOST // 2))
    slot_ref[...] = slot
    step = 256
    for first in range(0, total, step):
        chosen_ref[first : first + step, :] = bits(iota((step, rows), 0) + first == slot)
    rows_copy.wait()
    folded = jnp.zeros((rows, 128), jnp.float32)
    for left in range(0, rows_ref.shape[1], 128):
        values = rows_ref[:, left : left + 128].astype(jnp.float32)
        folded = folded + values * values
    scale = lax.rsqrt(jnp.sum(folded, axis=1, keepdims=True) + 1e-06)
    for left in range(0, rows_ref.shape[1], step):
        unit = rows_ref[:, left : left + step].astype(jnp.float32) * scale
        if left == 0:
            unit = jnp.where((jnp.abs(unit) < MARK) & (iota(unit.shape, 1) == 0), MARK, unit)
        unit_ref[:, left : left + step] = unit.astype(jnp.bfloat16)
        placed = dot(chosen_ref[...], unit_ref[:, left : left + step], ((1,), (0,)))
        send_ref[:, left : left + step] = placed.astype(jnp.bfloat16)


def maxima_kernel(rows_ref, out_ref):
    total, width = rows_ref.shape
    count = out_ref.shape[0]
    half = total // CL_DEV
    step = 256
    blocks = half // step
    tile = 128
    upper = iota((16, width), 0) & MOST == 0
    groups = [rows_ref[first : first + 16, :] for first in range(0, total, 16)]
    pairs = list(zip(groups[::2], groups[1::2]))
    sides = [
        jnp.concatenate([jnp.where(upper, one, two) for one, two in pairs], axis=0),
        jnp.concatenate([jnp.where(upper, two, one) for one, two in pairs], axis=0),
    ]
    other = iota((step, step), 0) != iota((step, step), 1)
    found = []
    for held in sides:
        mark = [held[b * step : (b + 1) * step, :tile].astype(jnp.float32) for b in range(blocks)]
        down = [jnp.where(m[:, :1] != 0.0, 0.0, LOW) for m in mark]
        across = [jnp.where(jnp.transpose(m)[:1] != 0.0, 0.0, LOW) for m in mark]
        over_rows = [jnp.full((8, step), -1.0, jnp.float32) for _ in range(blocks)]
        over_columns = [jnp.full((step, tile), -1.0, jnp.float32) for _ in range(blocks)]
        for i in range(blocks):
            for j in range(i, blocks):
                sim = dot(held[i * step : (i + 1) * step, :], held[j * step : (j + 1) * step, :], ((1,), (1,)))
                sim = sim + down[i]
                if i == j:
                    sim = jnp.where(other, sim, LOW)
                else:
                    sim = sim + across[j]
                    for first in range(0, step, tile):
                        over_columns[i] = jnp.maximum(over_columns[i], sim[:, first : first + tile])
                over_rows[j] = jnp.maximum(over_rows[j], jnp.max(sim.reshape(step // 8, 8, step), axis=0))
        best = []
        for over_row, over_column in zip(over_rows, over_columns):
            column = jnp.max(jnp.transpose(over_column), axis=0, keepdims=True)
            best.append(jnp.maximum(jnp.max(over_row, axis=0, keepdims=True), column))
        tiles = [row[:, first : first + tile] for row in best for first in range(0, step, tile)]
        found.append(jnp.concatenate([t for row in tiles for t in (row, pltpu.roll(row, tile // 2, axis=1))], axis=0))
    first_half = iota(found[0].shape, 1) & MOST == 0
    lines = found[0].shape[0]
    apart = count // lines
    for swap in range(CL_DEV):
        best = jnp.where(first_half, found[swap], found[1 - swap])
        for place in range(tile // 2 // PART):
            row = place // 2 * 4 + swap * 2 + place % 2
            out_ref[pl.ds(row, lines, stride=apart), :] = pltpu.roll(best, -place * PART % tile, axis=1)


def lookup_kernel(slot_ref, found_ref, out_ref):
    rows = slot_ref.shape[1]
    count = found_ref.shape[0]
    slot = slot_ref[...]
    owner = bits(iota((count, rows), 0) == slot // PART)
    found = jnp.concatenate(parts_of(jnp.transpose(found_ref[...])[:PART]), axis=0)
    picked = dot(found, owner, ((1,), (0,)))
    picked = picked[:PART] + picked[PART:]
    out_ref[...] = jnp.sum(jnp.where(iota((PART, rows), 0) == slot % PART, picked, 0.0), axis=0, keepdims=True)


def call(kernel, out_shape, name):
    return pl.pallas_call(
        kernel,
        out_shape=out_shape,
        compiler_params=PARAMS,
        name=name,
    )


def exchange(array):
    return lax.all_to_all(array, "work", split_axis=0, concat_axis=0, tiled=True)


def local(embeddings, labels):
    count = lax.axis_size("work")
    rows, width = embeddings.shape
    total = count * PART
    send, slot = pl.pallas_call(
        place_kernel,
        out_shape=(jax.ShapeDtypeStruct((total, width), jnp.bfloat16), jax.ShapeDtypeStruct((1, rows), jnp.int32)),
        in_specs=[pl.BlockSpec(memory_space=pltpu.HBM)] * 2,
        scratch_shapes=[
            pltpu.VMEM((1, rows), jnp.int32),
            pltpu.VMEM((rows, width), jnp.bfloat16),
            pltpu.VMEM((rows, width), jnp.bfloat16),
            pltpu.VMEM((total, rows), jnp.bfloat16),
            pltpu.SemaphoreType.DMA,
            pltpu.SemaphoreType.DMA,
        ],
        compiler_params=PARAMS,
        name="place",
    )(
        pltpu.with_memory_space_constraint(labels.reshape(1, rows), pltpu.HBM),
        pltpu.with_memory_space_constraint(embeddings, pltpu.HBM),
    )
    held = exchange(send.reshape(count, PART, width)).reshape(total, width)
    best = call(maxima_kernel, jax.ShapeDtypeStruct((count, 128), jnp.float32), "maxima")(held)
    found = exchange(best)
    nearest = call(lookup_kernel, jax.ShapeDtypeStruct((1, rows), jnp.float32), "lookup")(slot, found)
    return nearest.reshape(rows)


def solution(mesh):
    return jax.shard_map(
        local,
        mesh=mesh,
        in_specs=(P("work", None), P("work", None)),
        out_specs=P("work"),
        check_vma=False,
    )
```

```python
import jax
import jax.numpy as jnp
from jax import lax
from jax.experimental import pallas as pl
from jax.experimental.pallas import tpu as pltpu
from jax.sharding import PartitionSpec as P

CLUSTERS = 256
CL_DEV = 2
MOST = 4
PART = CL_DEV * MOST
MARK = 2.0**-126
LOW = -1e30
PARAMS = pltpu.CompilerParams(vmem_limit_bytes=40 * 1024 * 1024)


def iota(shape, dim):
    return lax.broadcasted_iota(jnp.int32, shape, dim)


def parts_of(values):
    out = []
    for _ in range(2):
        part = values.astype(jnp.bfloat16)
        out.append(part)
        values = values - part.astype(jnp.float32)
    return out


def bits(mask):
    return mask.astype(jnp.float32).astype(jnp.bfloat16)


def dot(a, b, dims):
    return lax.dot_general(a, b, (dims, ((), ())), preferred_element_type=jnp.float32)


def place_kernel(label_hbm, rows_hbm, send_ref, slot_ref, label_ref, rows_ref, chosen_ref, label_sem, rows_sem):
    rows = rows_ref.shape[0]
    total = send_ref.shape[0]
    label_copy = pltpu.make_async_copy(label_hbm, label_ref, label_sem)
    label_copy.start()
    rows_copy = pltpu.make_async_copy(rows_hbm, rows_ref, rows_sem)
    rows_copy.start()
    before = bits(iota((rows, rows), 0) < iota((rows, rows), 1))
    label_copy.wait()
    label = label_ref[...]
    member = iota((CLUSTERS, rows), 0) == label
    earlier = dot(bits(member), before, ((1,), (0,)))
    rank = jnp.sum(jnp.where(member, earlier, 0.0), axis=0, keepdims=True)
    slot = (label * MOST + rank.astype(jnp.int32)) ^ ((lax.axis_index("work") & 2) * (MOST // 2))
    slot_ref[...] = slot
    step = 256
    for first in range(0, total, step):
        chosen_ref[first : first + step, :] = bits(iota((step, rows), 0) + first == slot)
    rows_copy.wait()
    head = rows_ref[:, :128].astype(jnp.float32)
    head = jnp.where((jnp.abs(head) < MARK) & (iota(head.shape, 1) == 0), MARK, head)
    rows_ref[:, :128] = head.astype(jnp.bfloat16)
    for left in range(0, rows_ref.shape[1], step):
        placed = dot(chosen_ref[...], rows_ref[:, left : left + step], ((1,), (0,)))
        send_ref[:, left : left + step] = placed.astype(jnp.bfloat16)


def maxima_kernel(rows_ref, out_ref):
    total, width = rows_ref.shape
    count = out_ref.shape[0]
    half = total // CL_DEV
    step = 256
    blocks = half // step
    tile = 128
    upper = iota((16, width), 0) & MOST == 0
    groups = [rows_ref[first : first + 16, :] for first in range(0, total, 16)]
    pairs = list(zip(groups[::2], groups[1::2]))
    sides = [
        jnp.concatenate([jnp.where(upper, one, two) for one, two in pairs], axis=0),
        jnp.concatenate([jnp.where(upper, two, one) for one, two in pairs], axis=0),
    ]
    other = iota((step, step), 0) != iota((step, step), 1)
    found = []
    for held in sides:
        mark = [held[b * step : (b + 1) * step, :tile].astype(jnp.float32) for b in range(blocks)]
        down = [jnp.where(m[:, :1] != 0.0, 0.0, LOW) for m in mark]
        across = [jnp.where(jnp.transpose(m)[:1] != 0.0, 0.0, LOW) for m in mark]
        sims = {}
        for i in range(blocks):
            for j in range(i, blocks):
                sims[i, j] = dot(held[i * step : (i + 1) * step, :], held[j * step : (j + 1) * step, :], ((1,), (1,)))
        own = [jnp.where(other, 0.0, sims[b, b]) for b in range(blocks)]
        scale_down = [lax.rsqrt(jnp.sum(o, axis=1, keepdims=True) + 1e-06) for o in own]
        scale_across = [lax.rsqrt(jnp.sum(o, axis=0, keepdims=True) + 1e-06) for o in own]
        over_rows = [jnp.full((8, step), LOW, jnp.float32) for _ in range(blocks)]
        over_columns = [jnp.full((step, tile), LOW, jnp.float32) for _ in range(blocks)]
        for i, j in sims:
            sim = sims[i, j] * scale_down[i] + down[i]
            if i == j:
                sim = jnp.where(other, sim, LOW)
            else:
                turned = sims[i, j] * scale_across[j] + across[j]
                for first in range(0, step, tile):
                    over_columns[i] = jnp.maximum(over_columns[i], turned[:, first : first + tile])
            over_rows[j] = jnp.maximum(over_rows[j], jnp.max(sim.reshape(step // 8, 8, step), axis=0))
        best = []
        for over_row, over_column, scale in zip(over_rows, over_columns, scale_across):
            column = jnp.max(jnp.transpose(over_column), axis=0, keepdims=True)
            row = jnp.maximum(jnp.max(over_row, axis=0, keepdims=True), column)
            best.append(jnp.maximum(row * scale, -1.0))
        tiles = [row[:, first : first + tile] for row in best for first in range(0, step, tile)]
        found.append(jnp.concatenate([t for row in tiles for t in (row, pltpu.roll(row, tile // 2, axis=1))], axis=0))
    first_half = iota(found[0].shape, 1) & MOST == 0
    lines = found[0].shape[0]
    apart = count // lines
    for swap in range(CL_DEV):
        best = jnp.where(first_half, found[swap], found[1 - swap])
        for place in range(tile // 2 // PART):
            row = place // 2 * 4 + swap * 2 + place % 2
            out_ref[pl.ds(row, lines, stride=apart), :] = pltpu.roll(best, -place * PART % tile, axis=1)


def lookup_kernel(slot_ref, found_ref, out_ref):
    rows = slot_ref.shape[1]
    count = found_ref.shape[0]
    slot = slot_ref[...]
    owner = bits(iota((count, rows), 0) == slot // PART)
    found = jnp.concatenate(parts_of(jnp.transpose(found_ref[...])[:PART]), axis=0)
    picked = dot(found, owner, ((1,), (0,)))
    picked = picked[:PART] + picked[PART:]
    out_ref[...] = jnp.sum(jnp.where(iota((PART, rows), 0) == slot % PART, picked, 0.0), axis=0, keepdims=True)


def call(kernel, out_shape, name):
    return pl.pallas_call(
        kernel,
        out_shape=out_shape,
        compiler_params=PARAMS,
        name=name,
    )


def exchange(array):
    return lax.all_to_all(array, "work", split_axis=0, concat_axis=0, tiled=True)


def local(embeddings, labels):
    count = lax.axis_size("work")
    rows, width = embeddings.shape
    total = count * PART
    send, slot = pl.pallas_call(
        place_kernel,
        out_shape=(jax.ShapeDtypeStruct((total, width), jnp.bfloat16), jax.ShapeDtypeStruct((1, rows), jnp.int32)),
        in_specs=[pl.BlockSpec(memory_space=pltpu.HBM)] * 2,
        scratch_shapes=[
            pltpu.VMEM((1, rows), jnp.int32),
            pltpu.VMEM((rows, width), jnp.bfloat16),
            pltpu.VMEM((total, rows), jnp.bfloat16),
            pltpu.SemaphoreType.DMA,
            pltpu.SemaphoreType.DMA,
        ],
        compiler_params=PARAMS,
        name="place",
    )(
        pltpu.with_memory_space_constraint(labels.reshape(1, rows), pltpu.HBM),
        pltpu.with_memory_space_constraint(embeddings, pltpu.HBM),
    )
    held = exchange(send.reshape(count, PART, width)).reshape(total, width)
    best = call(maxima_kernel, jax.ShapeDtypeStruct((count, 128), jnp.float32), "maxima")(held)
    found = exchange(best)
    nearest = call(lookup_kernel, jax.ShapeDtypeStruct((1, rows), jnp.float32), "lookup")(slot, found)
    return nearest.reshape(rows)


def solution(mesh):
    return jax.shard_map(
        local,
        mesh=mesh,
        in_specs=(P("work", None), P("work", None)),
        out_specs=P("work"),
        check_vma=False,
    )
```

```python
import jax
import jax.numpy as jnp
from jax import lax
from jax.experimental import pallas as pl
from jax.experimental.pallas import tpu as pltpu
from jax.sharding import PartitionSpec as P

CLUSTERS = 256
CL_DEV = 2
MOST = 4
PART = CL_DEV * MOST
MARK = 2.0**-126
LOW = -1e30
PARAMS = pltpu.CompilerParams(vmem_limit_bytes=40 * 1024 * 1024)


def iota(shape, dim):
    return lax.broadcasted_iota(jnp.int32, shape, dim)


def parts_of(values):
    out = []
    for _ in range(2):
        part = values.astype(jnp.bfloat16)
        out.append(part)
        values = values - part.astype(jnp.float32)
    return out


def bits(mask):
    return mask.astype(jnp.float32).astype(jnp.bfloat16)


def dot(a, b, dims):
    return lax.dot_general(a, b, (dims, ((), ())), preferred_element_type=jnp.float32)


def place_kernel(label_hbm, rows_hbm, send_ref, slot_ref, label_ref, rows_ref, unit_ref, chosen_ref, label_sem, rows_sem):
    rows = rows_ref.shape[0]
    total = send_ref.shape[0]
    label_copy = pltpu.make_async_copy(label_hbm, label_ref, label_sem)
    label_copy.start()
    rows_copy = pltpu.make_async_copy(rows_hbm, rows_ref, rows_sem)
    rows_copy.start()
    before = bits(iota((rows, rows), 0) < iota((rows, rows), 1))
    label_copy.wait()
    label = label_ref[...]
    member = iota((CLUSTERS, rows), 0) == label
    earlier = dot(bits(member), before, ((1,), (0,)))
    rank = jnp.sum(jnp.where(member, earlier, 0.0), axis=0, keepdims=True)
    slot = (label * MOST + rank.astype(jnp.int32)) ^ ((lax.axis_index("work") & 2) * (MOST // 2))
    slot_ref[...] = slot
    step = 256
    for first in range(0, total, step):
        chosen_ref[first : first + step, :] = bits(iota((step, rows), 0) + first == slot)
    rows_copy.wait()
    folded = jnp.zeros((rows, 128), jnp.float32)
    for left in range(0, rows_ref.shape[1], 128):
        values = rows_ref[:, left : left + 128].astype(jnp.float32)
        folded = folded + values * values
    scale = lax.rsqrt(jnp.sum(folded, axis=1, keepdims=True) + 1e-06)
    for left in range(0, rows_ref.shape[1], step):
        unit = rows_ref[:, left : left + step].astype(jnp.float32) * scale
        if left == 0:
            unit = jnp.where((jnp.abs(unit) < MARK) & (iota(unit.shape, 1) == 0), MARK, unit)
        unit_ref[:, left : left + step] = unit.astype(jnp.bfloat16)
        placed = dot(chosen_ref[...], unit_ref[:, left : left + step], ((1,), (0,)))
        send_ref[:, left : left + step] = placed.astype(jnp.bfloat16)


def maxima_kernel(rows_ref, out_ref):
    total, width = rows_ref.shape
    count = out_ref.shape[0]
    half = total // CL_DEV
    step = 256
    blocks = half // step
    tile = 128
    upper = iota((16, width), 0) & MOST == 0
    groups = [rows_ref[first : first + 16, :] for first in range(0, total, 16)]
    pairs = list(zip(groups[::2], groups[1::2]))
    sides = [
        jnp.concatenate([jnp.where(upper, one, two) for one, two in pairs], axis=0),
        jnp.concatenate([jnp.where(upper, two, one) for one, two in pairs], axis=0),
    ]
    other = iota((step, step), 0) != iota((step, step), 1)
    found = []
    for held in sides:
        mark = [held[b * step : (b + 1) * step, :tile].astype(jnp.float32) for b in range(blocks)]
        down = [jnp.where(m[:, :1] != 0.0, 0.0, LOW) for m in mark]
        across = [jnp.where(jnp.transpose(m)[:1] != 0.0, 0.0, LOW) for m in mark]
        over_rows = [jnp.full((8, step), -1.0, jnp.float32) for _ in range(blocks)]
        over_columns = [jnp.full((step, tile), -1.0, jnp.float32) for _ in range(blocks)]
        for j in reversed(range(blocks)):
            tall = dot(held[: (j + 1) * step, :], held[j * step : (j + 1) * step, :], ((1,), (1,)))
            for i in range(j + 1):
                sim = tall[i * step : (i + 1) * step] + down[i]
                if i == j:
                    sim = jnp.where(other, sim, LOW)
                else:
                    sim = sim + across[j]
                    for first in range(0, step, tile):
                        over_columns[i] = jnp.maximum(over_columns[i], sim[:, first : first + tile])
                over_rows[j] = jnp.maximum(over_rows[j], jnp.max(sim.reshape(step // 8, 8, step), axis=0))
        best = []
        for over_row, over_column in zip(over_rows, over_columns):
            column = jnp.max(jnp.transpose(over_column), axis=0, keepdims=True)
            best.append(jnp.maximum(jnp.max(over_row, axis=0, keepdims=True), column))
        tiles = [row[:, first : first + tile] for row in best for first in range(0, step, tile)]
        found.append(jnp.concatenate([t for row in tiles for t in (row, pltpu.roll(row, tile // 2, axis=1))], axis=0))
    first_half = iota(found[0].shape, 1) & MOST == 0
    lines = found[0].shape[0]
    apart = count // lines
    for swap in range(CL_DEV):
        best = jnp.where(first_half, found[swap], found[1 - swap])
        for place in range(tile // 2 // PART):
            row = place // 2 * 4 + swap * 2 + place % 2
            out_ref[pl.ds(row, lines, stride=apart), :] = pltpu.roll(best, -place * PART % tile, axis=1)


def lookup_kernel(slot_ref, found_ref, out_ref):
    rows = slot_ref.shape[1]
    count = found_ref.shape[0]
    slot = slot_ref[...]
    owner = bits(iota((count, rows), 0) == slot // PART)
    found = jnp.concatenate(parts_of(jnp.transpose(found_ref[...])[:PART]), axis=0)
    picked = dot(found, owner, ((1,), (0,)))
    picked = picked[:PART] + picked[PART:]
    out_ref[...] = jnp.sum(jnp.where(iota((PART, rows), 0) == slot % PART, picked, 0.0), axis=0, keepdims=True)


def call(kernel, out_shape, name):
    return pl.pallas_call(
        kernel,
        out_shape=out_shape,
        compiler_params=PARAMS,
        name=name,
    )


def exchange(array):
    return lax.all_to_all(array, "work", split_axis=0, concat_axis=0, tiled=True)


def local(embeddings, labels):
    count = lax.axis_size("work")
    rows, width = embeddings.shape
    total = count * PART
    send, slot = pl.pallas_call(
        place_kernel,
        out_shape=(jax.ShapeDtypeStruct((total, width), jnp.bfloat16), jax.ShapeDtypeStruct((1, rows), jnp.int32)),
        in_specs=[pl.BlockSpec(memory_space=pltpu.HBM)] * 2,
        scratch_shapes=[
            pltpu.VMEM((1, rows), jnp.int32),
            pltpu.VMEM((rows, width), jnp.bfloat16),
            pltpu.VMEM((rows, width), jnp.bfloat16),
            pltpu.VMEM((total, rows), jnp.bfloat16),
            pltpu.SemaphoreType.DMA,
            pltpu.SemaphoreType.DMA,
        ],
        compiler_params=PARAMS,
        name="place",
    )(
        pltpu.with_memory_space_constraint(labels.reshape(1, rows), pltpu.HBM),
        pltpu.with_memory_space_constraint(embeddings, pltpu.HBM),
    )
    held = exchange(send.reshape(count, PART, width)).reshape(total, width)
    best = call(maxima_kernel, jax.ShapeDtypeStruct((count, 128), jnp.float32), "maxima")(held)
    found = exchange(best)
    nearest = call(lookup_kernel, jax.ShapeDtypeStruct((1, rows), jnp.float32), "lookup")(slot, found)
    return nearest.reshape(rows)


def solution(mesh):
    return jax.shard_map(
        local,
        mesh=mesh,
        in_specs=(P("work", None), P("work", None)),
        out_specs=P("work"),
        check_vma=False,
    )
```

```python
import jax
import jax.numpy as jnp
from jax import lax
from jax.experimental import pallas as pl
from jax.experimental.pallas import tpu as pltpu
from jax.sharding import PartitionSpec as P

CLUSTERS = 256
CL_DEV = 2
MOST = 4
PART = CL_DEV * MOST
MARK = 2.0**-126
LOW = -1e30
PARAMS = pltpu.CompilerParams(vmem_limit_bytes=40 * 1024 * 1024)


def iota(shape, dim):
    return lax.broadcasted_iota(jnp.int32, shape, dim)


def parts_of(values):
    out = []
    for _ in range(2):
        part = values.astype(jnp.bfloat16)
        out.append(part)
        values = values - part.astype(jnp.float32)
    return out


def bits(mask):
    return mask.astype(jnp.float32).astype(jnp.bfloat16)


def dot(a, b, dims):
    return lax.dot_general(a, b, (dims, ((), ())), preferred_element_type=jnp.float32)


def place_kernel(label_hbm, rows_hbm, send_ref, slot_ref, label_ref, rows_ref, unit_ref, chosen_ref, label_sem, rows_sem):
    rows = rows_ref.shape[0]
    total = send_ref.shape[0]
    label_copy = pltpu.make_async_copy(label_hbm, label_ref, label_sem)
    label_copy.start()
    rows_copy = pltpu.make_async_copy(rows_hbm, rows_ref, rows_sem)
    rows_copy.start()
    before = bits(iota((rows, rows), 0) < iota((rows, rows), 1))
    label_copy.wait()
    label = label_ref[...]
    member = iota((CLUSTERS, rows), 0) == label
    earlier = dot(bits(member), before, ((1,), (0,)))
    rank = jnp.sum(jnp.where(member, earlier, 0.0), axis=0, keepdims=True)
    slot = (label * MOST + rank.astype(jnp.int32)) ^ ((lax.axis_index("work") & 2) * (MOST // 2))
    slot_ref[...] = slot
    step = 256
    for first in range(0, total, step):
        chosen_ref[first : first + step, :] = bits(iota((step, rows), 0) + first == slot)
    rows_copy.wait()
    folded = jnp.zeros((rows, 128), jnp.float32)
    for left in range(0, rows_ref.shape[1], 128):
        values = rows_ref[:, left : left + 128].astype(jnp.float32)
        folded = folded + values * values
    scale = lax.rsqrt(jnp.sum(folded, axis=1, keepdims=True) + 1e-06)
    for left in range(0, rows_ref.shape[1], step):
        unit = rows_ref[:, left : left + step].astype(jnp.float32) * scale
        if left == 0:
            unit = jnp.where((jnp.abs(unit) < MARK) & (iota(unit.shape, 1) == 0), MARK, unit)
        unit_ref[:, left : left + step] = unit.astype(jnp.bfloat16)
        placed = dot(chosen_ref[...], unit_ref[:, left : left + step], ((1,), (0,)))
        send_ref[:, left : left + step] = placed.astype(jnp.bfloat16)


def maxima_kernel(rows_ref, out_ref):
    total, width = rows_ref.shape
    count = out_ref.shape[0]
    half = total // CL_DEV
    step = 256
    blocks = half // step
    tile = 128
    upper = iota((16, width), 0) & MOST == 0
    groups = [rows_ref[first : first + 16, :] for first in range(0, total, 16)]
    pairs = list(zip(groups[::2], groups[1::2]))
    sides = [
        jnp.concatenate([jnp.where(upper, one, two) for one, two in pairs], axis=0),
        jnp.concatenate([jnp.where(upper, two, one) for one, two in pairs], axis=0),
    ]
    other = iota((step, step), 0) != iota((step, step), 1)
    found = []
    for held in sides:
        mark = [held[b * step : (b + 1) * step, :tile].astype(jnp.float32) for b in range(blocks)]
        down = [jnp.where(m[:, :1] != 0.0, 0.0, LOW) for m in mark]
        across = [jnp.where(jnp.transpose(m)[:1] != 0.0, 0.0, LOW) if b else None for b, m in enumerate(mark)]
        over_rows = [jnp.full((8, step), -1.0, jnp.float32) for _ in range(blocks)]
        over_columns = [jnp.full((step, tile), -1.0, jnp.float32) for _ in range(blocks)]
        for j in reversed(range(blocks)):
            tall = dot(held[: (j + 1) * step, :], held[j * step : (j + 1) * step, :], ((1,), (1,)))
            for i in range(j + 1):
                sim = tall[i * step : (i + 1) * step] + down[i]
                if i == j:
                    sim = jnp.where(other, sim, LOW)
                else:
                    sim = sim + across[j]
                    for first in range(0, step, tile):
                        over_columns[i] = jnp.maximum(over_columns[i], sim[:, first : first + tile])
                over_rows[j] = jnp.maximum(over_rows[j], jnp.max(sim.reshape(step // 8, 8, step), axis=0))
        best = []
        for b in range(blocks):
            row = jnp.max(over_rows[b], axis=0, keepdims=True)
            if b < blocks - 1:
                row = jnp.maximum(row, jnp.max(jnp.transpose(over_columns[b]), axis=0, keepdims=True))
            best.append(row)
        tiles = [row[:, first : first + tile] for row in best for first in range(0, step, tile)]
        found.append(jnp.concatenate([t for row in tiles for t in (row, pltpu.roll(row, tile // 2, axis=1))], axis=0))
    first_half = iota(found[0].shape, 1) & MOST == 0
    lines = found[0].shape[0]
    apart = count // lines
    for swap in range(CL_DEV):
        best = jnp.where(first_half, found[swap], found[1 - swap])
        for place in range(tile // 2 // PART):
            row = place // 2 * 4 + swap * 2 + place % 2
            out_ref[pl.ds(row, lines, stride=apart), :] = pltpu.roll(best, -place * PART % tile, axis=1)[:, :PART]


def lookup_kernel(slot_ref, found_ref, out_ref):
    rows = slot_ref.shape[1]
    count = found_ref.shape[0]
    slot = slot_ref[...]
    owner = bits(iota((count, rows), 0) == slot // PART)
    found = jnp.concatenate(parts_of(jnp.transpose(found_ref[...])), axis=0)
    picked = dot(found, owner, ((1,), (0,)))
    picked = picked[:PART] + picked[PART:]
    out_ref[...] = jnp.sum(jnp.where(iota((PART, rows), 0) == slot % PART, picked, 0.0), axis=0, keepdims=True)


def call(kernel, out_shape, name):
    return pl.pallas_call(
        kernel,
        out_shape=out_shape,
        compiler_params=PARAMS,
        name=name,
    )


def exchange(array):
    return lax.all_to_all(array, "work", split_axis=0, concat_axis=0, tiled=True)


def local(embeddings, labels):
    count = lax.axis_size("work")
    rows, width = embeddings.shape
    total = count * PART
    send, slot = pl.pallas_call(
        place_kernel,
        out_shape=(jax.ShapeDtypeStruct((total, width), jnp.bfloat16), jax.ShapeDtypeStruct((1, rows), jnp.int32)),
        in_specs=[pl.BlockSpec(memory_space=pltpu.HBM)] * 2,
        scratch_shapes=[
            pltpu.VMEM((1, rows), jnp.int32),
            pltpu.VMEM((rows, width), jnp.bfloat16),
            pltpu.VMEM((rows, width), jnp.bfloat16),
            pltpu.VMEM((total, rows), jnp.bfloat16),
            pltpu.SemaphoreType.DMA,
            pltpu.SemaphoreType.DMA,
        ],
        compiler_params=PARAMS,
        name="place",
    )(
        pltpu.with_memory_space_constraint(labels.reshape(1, rows), pltpu.HBM),
        pltpu.with_memory_space_constraint(embeddings, pltpu.HBM),
    )
    held = exchange(send.reshape(count, PART, width)).reshape(total, width)
    best = call(maxima_kernel, jax.ShapeDtypeStruct((count, PART), jnp.float32), "maxima")(held)
    found = exchange(best)
    nearest = call(lookup_kernel, jax.ShapeDtypeStruct((1, rows), jnp.float32), "lookup")(slot, found)
    return nearest.reshape(rows)


def solution(mesh):
    return jax.shard_map(
        local,
        mesh=mesh,
        in_specs=(P("work", None), P("work", None)),
        out_specs=P("work"),
        check_vma=False,
    )
```

```python
import jax
import jax.numpy as jnp
from jax import lax
from jax.experimental import pallas as pl
from jax.experimental.pallas import tpu as pltpu
from jax.sharding import PartitionSpec as P

CLUSTERS = 256
CL_DEV = 2
MOST = 4
PART = CL_DEV * MOST
MARK = 2.0**-126
LOW = -1e30
PARAMS = pltpu.CompilerParams(vmem_limit_bytes=40 * 1024 * 1024)


def iota(shape, dim):
    return lax.broadcasted_iota(jnp.int32, shape, dim)


def parts_of(values):
    out = []
    for _ in range(2):
        part = values.astype(jnp.bfloat16)
        out.append(part)
        values = values - part.astype(jnp.float32)
    return out


def bits(mask):
    return mask.astype(jnp.float32).astype(jnp.bfloat16)


def dot(a, b, dims):
    return lax.dot_general(a, b, (dims, ((), ())), preferred_element_type=jnp.float32)


def place_kernel(label_hbm, rows_hbm, send_ref, slot_ref, label_ref, rows_ref, unit_ref, chosen_ref, label_sem, rows_sem):
    rows = rows_ref.shape[0]
    total = send_ref.shape[0]
    label_copy = pltpu.make_async_copy(label_hbm, label_ref, label_sem)
    label_copy.start()
    rows_copy = pltpu.make_async_copy(rows_hbm, rows_ref, rows_sem)
    rows_copy.start()
    before = bits(iota((rows, rows), 0) < iota((rows, rows), 1))
    label_copy.wait()
    label = label_ref[...]
    member = iota((CLUSTERS, rows), 0) == label
    earlier = dot(bits(member), before, ((1,), (0,)))
    rank = jnp.sum(jnp.where(member, earlier, 0.0), axis=0, keepdims=True)
    slot = (label * MOST + rank.astype(jnp.int32)) ^ ((lax.axis_index("work") & 2) * (MOST // 2))
    slot_ref[...] = slot
    step = 256
    for first in range(0, total, step):
        chosen_ref[first : first + step, :] = bits(iota((step, rows), 0) + first == slot)
    rows_copy.wait()
    folded = jnp.zeros((rows, 128), jnp.float32)
    for left in range(0, rows_ref.shape[1], 128):
        values = rows_ref[:, left : left + 128].astype(jnp.float32)
        folded = folded + values * values
    scale = lax.rsqrt(jnp.sum(folded, axis=1, keepdims=True) + 1e-06)
    for left in reversed(range(0, rows_ref.shape[1], step)):
        unit = rows_ref[:, left : left + step].astype(jnp.float32) * scale
        if left == 0:
            head = unit[:, :128]
            head = jnp.where((jnp.abs(head) < MARK) & (iota(head.shape, 1) == 0), MARK, head)
            unit = jnp.concatenate([head, unit[:, 128:]], axis=1)
        unit_ref[:, left : left + step] = unit.astype(jnp.bfloat16)
        placed = dot(chosen_ref[...], unit_ref[:, left : left + step], ((1,), (0,)))
        send_ref[:, left : left + step] = placed.astype(jnp.bfloat16)


def maxima_kernel(rows_ref, out_ref):
    total, width = rows_ref.shape
    count = out_ref.shape[0]
    half = total // CL_DEV
    step = 256
    blocks = half // step
    tile = 128
    upper = iota((16, width), 0) & MOST == 0
    groups = [rows_ref[first : first + 16, :] for first in range(0, total, 16)]
    pairs = list(zip(groups[::2], groups[1::2]))
    sides = [
        jnp.concatenate([jnp.where(upper, one, two) for one, two in pairs], axis=0),
        jnp.concatenate([jnp.where(upper, two, one) for one, two in pairs], axis=0),
    ]
    other = iota((step, step), 0) != iota((step, step), 1)
    found = []
    for held in sides:
        mark = [held[b * step : (b + 1) * step, :tile].astype(jnp.float32) for b in range(blocks)]
        down = [jnp.where(m[:, :1] != 0.0, 0.0, LOW) for m in mark]
        across = [jnp.where(jnp.transpose(m)[:1] != 0.0, 0.0, LOW) for m in mark]
        over_rows = [jnp.full((8, step), -1.0, jnp.float32) for _ in range(blocks)]
        over_columns = [jnp.full((step, tile), -1.0, jnp.float32) for _ in range(blocks)]
        for j in reversed(range(blocks)):
            tall = dot(held[: (j + 1) * step, :], held[j * step : (j + 1) * step, :], ((1,), (1,)))
            for i in range(j + 1):
                sim = tall[i * step : (i + 1) * step] + down[i]
                if i == j:
                    sim = jnp.where(other, sim, LOW)
                else:
                    sim = sim + across[j]
                    for first in range(0, step, tile):
                        over_columns[i] = jnp.maximum(over_columns[i], sim[:, first : first + tile])
                over_rows[j] = jnp.maximum(over_rows[j], jnp.max(sim.reshape(step // 8, 8, step), axis=0))
        best = []
        for over_row, over_column in zip(over_rows, over_columns):
            column = jnp.max(jnp.transpose(over_column), axis=0, keepdims=True)
            best.append(jnp.maximum(jnp.max(over_row, axis=0, keepdims=True), column))
        tiles = [row[:, first : first + tile] for row in best for first in range(0, step, tile)]
        found.append(jnp.concatenate([t for row in tiles for t in (row, pltpu.roll(row, tile // 2, axis=1))], axis=0))
    first_half = iota(found[0].shape, 1) & MOST == 0
    lines = found[0].shape[0]
    apart = count // lines
    for swap in range(CL_DEV):
        best = jnp.where(first_half, found[swap], found[1 - swap])
        for place in range(tile // 2 // PART):
            row = place // 2 * 4 + swap * 2 + place % 2
            out_ref[pl.ds(row, lines, stride=apart), :] = pltpu.roll(best, -place * PART % tile, axis=1)


def lookup_kernel(slot_ref, found_ref, out_ref):
    rows = slot_ref.shape[1]
    count = found_ref.shape[0]
    slot = slot_ref[...]
    owner = bits(iota((count, rows), 0) == slot // PART)
    found = jnp.concatenate(parts_of(jnp.transpose(found_ref[...])[:PART]), axis=0)
    picked = dot(found, owner, ((1,), (0,)))
    picked = picked[:PART] + picked[PART:]
    out_ref[...] = jnp.sum(jnp.where(iota((PART, rows), 0) == slot % PART, picked, 0.0), axis=0, keepdims=True)


def call(kernel, out_shape, name):
    return pl.pallas_call(
        kernel,
        out_shape=out_shape,
        compiler_params=PARAMS,
        name=name,
    )


def exchange(array):
    return lax.all_to_all(array, "work", split_axis=0, concat_axis=0, tiled=True)


def local(embeddings, labels):
    count = lax.axis_size("work")
    rows, width = embeddings.shape
    total = count * PART
    send, slot = pl.pallas_call(
        place_kernel,
        out_shape=(jax.ShapeDtypeStruct((total, width), jnp.bfloat16), jax.ShapeDtypeStruct((1, rows), jnp.int32)),
        in_specs=[pl.BlockSpec(memory_space=pltpu.HBM)] * 2,
        scratch_shapes=[
            pltpu.VMEM((1, rows), jnp.int32),
            pltpu.VMEM((rows, width), jnp.bfloat16),
            pltpu.VMEM((rows, width), jnp.bfloat16),
            pltpu.VMEM((total, rows), jnp.bfloat16),
            pltpu.SemaphoreType.DMA,
            pltpu.SemaphoreType.DMA,
        ],
        compiler_params=PARAMS,
        name="place",
    )(
        pltpu.with_memory_space_constraint(labels.reshape(1, rows), pltpu.HBM),
        pltpu.with_memory_space_constraint(embeddings, pltpu.HBM),
    )
    held = exchange(send.reshape(count, PART, width)).reshape(total, width)
    best = call(maxima_kernel, jax.ShapeDtypeStruct((count, 128), jnp.float32), "maxima")(held)
    found = exchange(best)
    nearest = call(lookup_kernel, jax.ShapeDtypeStruct((1, rows), jnp.float32), "lookup")(slot, found)
    return nearest.reshape(rows)


def solution(mesh):
    return jax.shard_map(
        local,
        mesh=mesh,
        in_specs=(P("work", None), P("work", None)),
        out_specs=P("work"),
        check_vma=False,
    )
```

```python
import jax
import jax.numpy as jnp
from jax import lax
from jax.experimental import pallas as pl
from jax.experimental.pallas import tpu as pltpu
from jax.sharding import PartitionSpec as P

CLUSTERS = 256
CL_DEV = 2
MOST = 4
PART = CL_DEV * MOST
MARK = 2.0**-126
LOW = -1e30
PARAMS = pltpu.CompilerParams(vmem_limit_bytes=40 * 1024 * 1024)


def iota(shape, dim):
    return lax.broadcasted_iota(jnp.int32, shape, dim)


def parts_of(values):
    out = []
    for _ in range(2):
        part = values.astype(jnp.bfloat16)
        out.append(part)
        values = values - part.astype(jnp.float32)
    return out


def bits(mask):
    return mask.astype(jnp.float32).astype(jnp.bfloat16)


def dot(a, b, dims):
    return lax.dot_general(a, b, (dims, ((), ())), preferred_element_type=jnp.float32)


def place_kernel(label_hbm, rows_hbm, send_ref, slot_ref, label_ref, rows_ref, unit_ref, chosen_ref, label_sem, rows_sem):
    rows = rows_ref.shape[0]
    total = send_ref.shape[0]
    label_copy = pltpu.make_async_copy(label_hbm, label_ref, label_sem)
    label_copy.start()
    rows_copy = pltpu.make_async_copy(rows_hbm, rows_ref, rows_sem)
    rows_copy.start()
    before = bits(iota((rows, rows), 0) < iota((rows, rows), 1))
    label_copy.wait()
    label = label_ref[...]
    member = iota((CLUSTERS, rows), 0) == label
    earlier = dot(bits(member), before, ((1,), (0,)))
    rank = jnp.sum(jnp.where(member, earlier, 0.0), axis=0, keepdims=True)
    slot = (label * MOST + rank.astype(jnp.int32)) ^ ((lax.axis_index("work") & 2) * (MOST // 2))
    slot_ref[...] = slot
    step = 256
    for first in range(0, total, step):
        chosen_ref[first : first + step, :] = bits(iota((step, rows), 0) + first == slot)
    rows_copy.wait()
    folded = jnp.zeros((rows, 128), jnp.float32)
    for left in range(0, rows_ref.shape[1], 128):
        values = rows_ref[:, left : left + 128].astype(jnp.float32)
        folded = folded + values * values
    scale = lax.rsqrt(jnp.sum(folded, axis=1, keepdims=True) + 1e-06)
    for left in reversed(range(0, rows_ref.shape[1], step)):
        unit = rows_ref[:, left : left + step].astype(jnp.float32) * scale
        if left == 0:
            head = unit[:, :128]
            head = jnp.where((jnp.abs(head) < MARK) & (iota(head.shape, 1) == 0), MARK, head)
            unit = jnp.concatenate([head, unit[:, 128:]], axis=1)
        unit_ref[:, left : left + step] = unit.astype(jnp.bfloat16)
        placed = dot(chosen_ref[...], unit_ref[:, left : left + step], ((1,), (0,)))
        send_ref[:, left : left + step] = placed.astype(jnp.bfloat16)


def maxima_kernel(rows_ref, out_ref):
    total, width = rows_ref.shape
    count = out_ref.shape[0]
    half = total // CL_DEV
    step = 256
    blocks = half // step
    tile = 128
    upper = iota((16, width), 0) & MOST == 0
    groups = [rows_ref[first : first + 16, :] for first in range(0, total, 16)]
    pairs = list(zip(groups[::2], groups[1::2]))
    sides = [
        jnp.concatenate([jnp.where(upper, one, two) for one, two in pairs], axis=0),
        jnp.concatenate([jnp.where(upper, two, one) for one, two in pairs], axis=0),
    ]
    other = iota((step, step), 0) != iota((step, step), 1)
    found = []
    for held in sides:
        mark = [held[b * step : (b + 1) * step, :tile].astype(jnp.float32) for b in range(blocks)]
        down = [jnp.where(m[:, :1] != 0.0, 0.0, LOW) for m in mark]
        across = [jnp.where(jnp.transpose(m)[:1] != 0.0, 0.0, LOW) if b else None for b, m in enumerate(mark)]
        over_rows = [jnp.full((8, step), -1.0, jnp.float32) for _ in range(blocks)]
        over_columns = [jnp.full((step, tile), -1.0, jnp.float32) for _ in range(blocks)]
        for j in reversed(range(blocks)):
            tall = dot(held[: (j + 1) * step, :], held[j * step : (j + 1) * step, :], ((1,), (1,)))
            for i in range(j + 1):
                sim = tall[i * step : (i + 1) * step] + down[i]
                if i == j:
                    sim = jnp.where(other, sim, LOW)
                else:
                    sim = sim + across[j]
                    for first in range(0, step, tile):
                        over_columns[i] = jnp.maximum(over_columns[i], sim[:, first : first + tile])
                over_rows[j] = jnp.maximum(over_rows[j], jnp.max(sim.reshape(step // 8, 8, step), axis=0))
        best = []
        for b in range(blocks):
            row = jnp.max(over_rows[b], axis=0, keepdims=True)
            if b < blocks - 1:
                row = jnp.maximum(row, jnp.max(jnp.transpose(over_columns[b]), axis=0, keepdims=True))
            best.append(row)
        tiles = [row[:, first : first + tile] for row in best for first in range(0, step, tile)]
        found.append(jnp.concatenate([t for row in tiles for t in (row, pltpu.roll(row, tile // 2, axis=1))], axis=0))
    first_half = iota(found[0].shape, 1) & MOST == 0
    lines = found[0].shape[0]
    apart = count // lines
    for swap in range(CL_DEV):
        best = jnp.where(first_half, found[swap], found[1 - swap])
        for place in range(tile // 2 // PART):
            row = place // 2 * 4 + swap * 2 + place % 2
            out_ref[pl.ds(row, lines, stride=apart), :] = pltpu.roll(best, -place * PART % tile, axis=1)


def lookup_kernel(slot_ref, found_ref, out_ref):
    rows = slot_ref.shape[1]
    count = found_ref.shape[0]
    slot = slot_ref[...]
    owner = bits(iota((count, rows), 0) == slot // PART)
    found = jnp.concatenate(parts_of(jnp.transpose(found_ref[...])[:PART]), axis=0)
    picked = dot(found, owner, ((1,), (0,)))
    picked = picked[:PART] + picked[PART:]
    out_ref[...] = jnp.sum(jnp.where(iota((PART, rows), 0) == slot % PART, picked, 0.0), axis=0, keepdims=True)


def call(kernel, out_shape, name):
    return pl.pallas_call(
        kernel,
        out_shape=out_shape,
        compiler_params=PARAMS,
        name=name,
    )


def exchange(array):
    return lax.all_to_all(array, "work", split_axis=0, concat_axis=0, tiled=True)


def local(embeddings, labels):
    count = lax.axis_size("work")
    rows, width = embeddings.shape
    total = count * PART
    send, slot = pl.pallas_call(
        place_kernel,
        out_shape=(jax.ShapeDtypeStruct((total, width), jnp.bfloat16), jax.ShapeDtypeStruct((1, rows), jnp.int32)),
        in_specs=[pl.BlockSpec(memory_space=pltpu.HBM)] * 2,
        scratch_shapes=[
            pltpu.VMEM((1, rows), jnp.int32),
            pltpu.VMEM((rows, width), jnp.bfloat16),
            pltpu.VMEM((rows, width), jnp.bfloat16),
            pltpu.VMEM((total, rows), jnp.bfloat16),
            pltpu.SemaphoreType.DMA,
            pltpu.SemaphoreType.DMA,
        ],
        compiler_params=PARAMS,
        name="place",
    )(
        pltpu.with_memory_space_constraint(labels.reshape(1, rows), pltpu.HBM),
        pltpu.with_memory_space_constraint(embeddings, pltpu.HBM),
    )
    held = exchange(send.reshape(count, PART, width)).reshape(total, width)
    best = call(maxima_kernel, jax.ShapeDtypeStruct((count, 128), jnp.float32), "maxima")(held)
    found = exchange(best)
    nearest = call(lookup_kernel, jax.ShapeDtypeStruct((1, rows), jnp.float32), "lookup")(slot, found)
    return nearest.reshape(rows)


def solution(mesh):
    return jax.shard_map(
        local,
        mesh=mesh,
        in_specs=(P("work", None), P("work", None)),
        out_specs=P("work"),
        check_vma=False,
    )
```
